32 devices in a mesh: ctx: 8 (over z, y), head: 4 (over x, core).
Axes of the slice: x: 2, y: 2, z: 4, core: 2. Of those that a mesh axis runs over, the one named last changes fastest.
Arguments:
- long_q: bfloat16 [4096, 8192], P(('ctx', 'head')), may hold values from -5 to 5
- long_kv: bfloat16 [4096, 2048], P(('ctx', 'head')), may hold values from -5 to 5
- long_lengths: int32 [4], replicated, may hold values from 1 to 2048, 4096 in all
- short_q: bfloat16 [1024, 8192], P(('ctx', 'head')), may hold values from -5 to 5
- short_kv: bfloat16 [1024, 2048], P(('ctx', 'head')), may hold values from -5 to 5
- short_docs: int32 [32, 32], P('ctx'), may hold values from 0 to 3, never falling along the last dimension, each value on 1 to 16 neighbouring positions
- short_dest: int32 [8, 4], P('ctx'), may hold values from 0 to 7, as said below
Outputs:
- long_out: bfloat16 [4096, 8192], P(('ctx', 'head'))
- short_out: bfloat16 [2048, 8192], P('ctx', 'head')
The draws below stay inside these ranges and needn't reach their ends.
Inputs may be any that keep to these rules, and one draw needn't show every extreme that they name: `long_lengths`: they sum to 4096; the largest is exactly 2048. `short_docs`: each row of 32 positions holds documents 0 to 3 in order, each of 1 to 16 positions, one of exactly 16. `short_dest`: row s lists the destinations of the 4 groups of ctx index s; the entries of a row are all different.
All inputs are finite; a program needn't handle non-finite values.
Results may differ from the reference program's by a relative error of at most 0.0065.
Values may be sent and summed in bfloat16 or wider, within the bound.
A program may use at most 128 MiB of HBM per device.

```python
import math
import jax
import jax.numpy as jnp
import numpy as np
from jax import lax

H = 64
KV = 8
HD = 128
LONG_DEV = 512
LSPAN = 4
SCAP = 32
SDOCS = 4
SMAX = 16
LMAX = 2048
LONG_TOK = 4096
LDOCS = 4
SGROUPS = 4
SHORT_TOK = 1024
N_CTX = 8


def query_draw(key, salt, row_count):
    key = jax.random.fold_in(key, salt + 1)
    values = jnp.clip(jax.random.normal(key, (row_count, H * HD), jnp.float32), -5.0, 5.0)
    return values.astype(jnp.bfloat16)


def pair_draw(key, salt, row_count):
    key = jax.random.fold_in(key, salt + 2)
    values = jnp.clip(jax.random.normal(key, (row_count, 2 * KV * HD), jnp.float32), -5.0, 5.0)
    return values.astype(jnp.bfloat16)


def draw_long_q(key, part):
    return query_draw(key, 71, LONG_TOK)


def draw_long_kv(key, part):
    return pair_draw(key, 71, LONG_TOK)


def draw_short_q(key, part):
    return query_draw(key, 83, SHORT_TOK)


def draw_short_kv(key, part):
    return pair_draw(key, 83, SHORT_TOK)


def draw_short_dest(key, part):
    key = jax.random.fold_in(key, 5)
    sub_keys = jax.random.split(key, N_CTX)
    listed = jax.vmap(lambda single: jax.random.permutation(single, N_CTX)[:SGROUPS])(sub_keys)
    return listed.astype(jnp.int32)


def length_profile(count, total, limit, slope):
    weights = [(1 << 20) // math.isqrt(grade ** slope) + 1 for grade in range(2, count + 1)]
    surplus, counts = total - limit - (count - 1), [1] * (count - 1)
    while surplus > 0:
        candidates = [i for i in range(count - 1) if counts[i] < limit]
        whole, remaining = sum([weights[i] for i in candidates]), surplus
        for i in candidates:
            more = min(limit - counts[i], max(1, remaining * weights[i] // whole), surplus)
            counts[i] = counts[i] + more
            surplus = surplus - more
    return np.array([limit] + counts)


def uneven(stream_key, count, total, limit, skew):
    if count == 2:
        one = jax.random.randint(stream_key, (), max(1, total - limit), min(limit, total - 1) + 1)
        return jnp.stack([one, total - one])
    lengths = jnp.asarray(length_profile(count, total, limit, skew), jnp.int32)
    twos = (count - 1) // 2
    source_of, taker = lengths[1:1 + 2 * twos:2], lengths[2:2 + 2 * twos:2]
    slack = jnp.minimum(source_of - 1, limit - taker)
    shifted = jax.random.randint(jax.random.fold_in(stream_key, 1), (twos,), 0, 1 << 20) % (slack + 1)
    lengths = lengths.at[1:1 + 2 * twos:2].set(source_of - shifted).at[2:2 + 2 * twos:2].set(taker + shifted)
    return lengths[jax.random.permutation(jax.random.fold_in(stream_key, 2), count)]


def setup_inputs(seed: int = 0) -> dict:
    keys = jax.random.split(jax.random.key(seed), 8)
    long_q = draw_long_q(jax.random.fold_in(keys[7], 71), 0)
    long_kv = draw_long_kv(jax.random.fold_in(keys[7], 71), 0)
    long_lengths = uneven(keys[2], LDOCS, LONG_TOK, LMAX, 2).astype(jnp.int32)
    short_q = draw_short_q(jax.random.fold_in(keys[7], 71), 0)
    short_kv = draw_short_kv(jax.random.fold_in(keys[7], 71), 0)
    short_docs = jax.vmap(lambda own: jnp.searchsorted(jnp.cumsum(uneven(own, SDOCS, SCAP, SMAX, 1)), jnp.arange(SCAP), side="right"))(jax.random.split(keys[5], (SHORT_TOK // SCAP))).reshape((SHORT_TOK // SCAP, SCAP)).astype(jnp.int32)
    short_dest = draw_short_dest(jax.random.fold_in(keys[7], 71), 0)
    return dict(long_q=long_q, long_kv=long_kv, long_lengths=long_lengths, short_q=short_q, short_kv=short_kv, short_docs=short_docs, short_dest=short_dest)


masked_score = -1.0e30


def doc_numbers(doc_ends, positions):
    return jnp.sum((positions[:, None] >= doc_ends[None, :]).astype(jnp.int32), axis=1)


def softmax_attend(queries, key_rows, value_rows, visible):
    scores = jnp.einsum('qgd,kd->qgk', queries.astype(jnp.float32), key_rows.astype(jnp.float32)) * (HD ** -0.5)
    scores = jnp.where(visible[:, None, :], scores, masked_score)
    row_top = jnp.max(scores, axis=-1, keepdims=True)
    weight = jnp.where(visible[:, None, :], jnp.exp(scores - row_top), 0.0)
    denominator = jnp.sum(weight, axis=-1)
    rounded = weight.astype(jnp.bfloat16)
    numerator = jnp.einsum('qgk,kd->qgd', rounded.astype(jnp.float32), value_rows.astype(jnp.float32))
    return (numerator / denominator[..., None]).astype(jnp.bfloat16)


def reference(long_q, long_kv, long_lengths, short_q, short_kv, short_docs, short_dest):
    group_size = H // KV
    span_rows = LONG_DEV
    window = (LSPAN + 1) * span_rows
    doc_ends = jnp.cumsum(long_lengths).astype(jnp.int32)
    padded_kv = jnp.concatenate([jnp.zeros((LSPAN * span_rows, 2 * KV * HD), jnp.bfloat16), long_kv], axis=0)

    def span(span_index):
        first_row = (span_index * span_rows).astype(jnp.int32)
        query_rows = lax.dynamic_slice_in_dim(long_q, first_row, span_rows, 0).reshape(span_rows, KV, group_size, HD)
        kv_rows = lax.dynamic_slice_in_dim(padded_kv, first_row, window, 0).reshape(window, KV, 2, HD)
        query_pos = first_row + jnp.arange(span_rows, dtype=jnp.int32)
        key_pos = first_row - LSPAN * span_rows + jnp.arange(window, dtype=jnp.int32)
        query_doc = doc_numbers(doc_ends, query_pos)
        key_doc = doc_numbers(doc_ends, key_pos)
        visible = (query_doc[:, None] == key_doc[None, :]) & (key_pos[None, :] <= query_pos[:, None]) & (key_pos[None, :] >= 0)

        def one_head(head_index):
            return softmax_attend(query_rows[:, head_index], kv_rows[:, head_index, 0], kv_rows[:, head_index, 1], visible)

        per_head = lax.map(one_head, jnp.arange(KV, dtype=jnp.int32))
        return jnp.transpose(per_head, (1, 0, 2, 3)).reshape(span_rows, H * HD)

    long_out = lax.map(span, jnp.arange(N_CTX, dtype=jnp.int32)).reshape(LONG_TOK, H * HD)

    groups = SHORT_TOK // SCAP
    query_groups = short_q.reshape(groups, SCAP, KV, group_size, HD)
    kv_groups = short_kv.reshape(groups, SCAP, KV, 2, HD)
    positions = jnp.arange(SCAP, dtype=jnp.int32)
    visible = (short_docs[:, :, None] == short_docs[:, None, :]) & (positions[None, None, :] <= positions[None, :, None])

    def group_attend(query_block, kv_block, group_mask):
        return jax.vmap(lambda queries, key_rows, value_rows: softmax_attend(queries, key_rows, value_rows, group_mask), in_axes=(1, 1, 1), out_axes=1)(query_block, kv_block[:, :, 0], kv_block[:, :, 1])

    attended = jax.vmap(group_attend)(query_groups, kv_groups, visible)
    attended = attended.reshape(N_CTX, SGROUPS, SCAP, H * HD).astype(jnp.float32)

    def target(destination):
        selector = (short_dest == destination).astype(jnp.float32)
        return jnp.einsum('sg,sgrc->src', selector, attended, precision=lax.Precision.HIGHEST).astype(jnp.bfloat16)

    short_out = lax.map(target, jnp.arange(N_CTX, dtype=jnp.int32)).reshape(N_CTX * N_CTX * SCAP, H * HD)
    return long_out, short_out
```

```python
import functools

import jax
import jax.numpy as jnp
from jax import lax
from jax.experimental import pallas as pl
from jax.experimental.pallas import tpu as pltpu
from jax.sharding import PartitionSpec as P

H = 64
KV = 8
HD = 128
SCAP = 32
LMAX = 2048
GROUP = H // KV
CHUNK = 128
BACK = 8
SLOTS = 2 * (BACK + 1)
WINDOW = SLOTS * CHUNK
LOG2E = 1.4426950408889634
EXP_SCALE = LOG2E * HD ** (-0.5)
masked_score = -1e30
MESH = pl.DeviceIdType.MESH
MIB = 1024 * 1024


def stacked_queries(q_ref, first_row, rows, first_head, heads):
    parts = [
        q_ref[first_row : first_row + rows, (first_head + g) * HD : (first_head + g + 1) * HD]
        for g in range(heads)
    ]
    return jnp.concatenate(parts, axis=0)


def attend(queries, keys, values, bias):
    scores = (
        lax.dot_general(
            queries, keys, (((1,), (1,)), ((), ())), preferred_element_type=jnp.float32
        )
        + bias
    )
    top = jnp.max(scores, axis=1, keepdims=True)
    weight = jnp.exp2((scores - top) * EXP_SCALE)
    total = jnp.sum(weight, axis=1, keepdims=True)
    out = jnp.dot(weight.astype(jnp.bfloat16), values, preferred_element_type=jnp.float32)
    return (out / total).astype(jnp.bfloat16)


def long_kernel(first_row_of, base_of, len_ref, q_ref, kv_ref, out_ref, bias_ref):
    rows = q_ref.shape[0]
    window = kv_ref.shape[0]

    @pl.when(pl.program_id(0) == 0)
    def _():
        query_pos = first_row_of() + lax.broadcasted_iota(jnp.int32, (rows, 1), 0)
        doc_start = jnp.zeros((rows, 1), jnp.int32)
        end = jnp.int32(0)
        for i in range(len_ref.shape[0]):
            end = end + len_ref[i]
            doc_start = jnp.where(query_pos >= end, end, doc_start)
        key_pos = base_of() + lax.broadcasted_iota(jnp.int32, (rows, window), 1)
        visible = (key_pos <= query_pos) & (key_pos >= doc_start)
        bias_ref[...] = jnp.where(visible, 0.0, masked_score)

    heads = 256 // rows
    keys = kv_ref[:, :HD]
    values = kv_ref[:, HD:]
    for block in range(GROUP // heads):
        first = block * heads
        queries = stacked_queries(q_ref, 0, rows, first, heads)
        bias = jnp.concatenate([bias_ref[...]] * heads, axis=0)
        out = attend(queries, keys, values, bias)
        for g in range(heads):
            out_ref[:, (first + g) * HD : (first + g + 1) * HD] = out[g * rows : (g + 1) * rows]


def long_attention(first_row_of, base_of, lengths, q, window):
    rows, keys = q.shape[0], window.shape[0]
    scores = H * rows * keys
    return pl.pallas_call(
        functools.partial(long_kernel, first_row_of, base_of),
        grid=(KV,),
        out_shape=jax.ShapeDtypeStruct(q.shape, jnp.bfloat16),
        in_specs=[
            pl.BlockSpec(memory_space=pltpu.SMEM),
            pl.BlockSpec((rows, GROUP * HD), lambda h: (0, h)),
            pl.BlockSpec((keys, 2 * HD), lambda h: (0, h)),
        ],
        out_specs=pl.BlockSpec((rows, GROUP * HD), lambda h: (0, h)),
        scratch_shapes=[pltpu.VMEM((rows, keys), jnp.float32)],
        compiler_params=pltpu.CompilerParams(vmem_limit_bytes=50 * MIB),
        cost_estimate=pl.CostEstimate(
            flops=4 * HD * scores, bytes_accessed=4 * q.size + 2 * window.size, transcendentals=scores
        ),
    )(lengths, q, window)


def short_kernel(q_ref, kv_ref, docs_ref, out_ref):
    groups = q_ref.shape[0] // SCAP
    first_group = lax.axis_index("head") * groups
    row = lax.broadcasted_iota(jnp.int32, (SCAP, SCAP), 0)
    col = lax.broadcasted_iota(jnp.int32, (SCAP, SCAP), 1)
    for j in range(groups):
        key_doc = jnp.broadcast_to(docs_ref[pl.ds(first_group + j, 1), :], (SCAP, SCAP))
        query_doc = jnp.sum(jnp.where(row == col, key_doc, 0), axis=1, keepdims=True)
        visible = (key_doc == query_doc) & (col <= row)
        bias = jnp.concatenate([jnp.where(visible, 0.0, masked_score)] * GROUP, axis=0)
        rows = slice(j * SCAP, (j + 1) * SCAP)
        for h in range(KV):
            out = attend(
                stacked_queries(q_ref, j * SCAP, SCAP, h * GROUP, GROUP),
                kv_ref[rows, 2 * h * HD : (2 * h + 1) * HD],
                kv_ref[rows, (2 * h + 1) * HD : (2 * h + 2) * HD],
                bias,
            )
            for g in range(GROUP):
                head = h * GROUP + g
                out_ref[rows, head * HD : (head + 1) * HD] = out[g * SCAP : (g + 1) * SCAP]


def short_attention(q, kv, docs):
    return pl.pallas_call(
        short_kernel,
        out_shape=jax.ShapeDtypeStruct(q.shape, jnp.bfloat16),
        in_specs=[pl.BlockSpec(memory_space=pltpu.VMEM)] * 3,
        out_specs=pl.BlockSpec(memory_space=pltpu.VMEM),
        compiler_params=pltpu.CompilerParams(vmem_limit_bytes=32 * MIB),
    )(q, kv, docs)


X0, X1, X2, Y0, Y1, Y2, Z1, Z2, D0, D1, D2, OWN = range(12)


def exchange_kernel(
    kv_ref, att_ref, dest_ref, win_ref, short_ref,
    gathered, outgoing,
    send_sem, recv_sem, pair_send, pair_recv, head_send, head_recv, ctx_send, ctx_recv,
    local_sem, fill_sem,
):
    ctx, head = lax.axis_index("ctx"), lax.axis_index("head")
    ctx_count, head_count = lax.axis_size("ctx"), lax.axis_size("head")
    z, y, x, c = ctx // 2, ctx % 2, head // 2, head % 2
    chip = ctx * 2 + x
    cols = gathered.shape[2]

    barrier = pltpu.get_barrier_semaphore()
    for k in range(1, head_count):
        pl.semaphore_signal(
            barrier, inc=1, device_id=(ctx, (head + k) % head_count), device_id_type=MESH
        )
    for k in range(1, ctx_count):
        pl.semaphore_signal(
            barrier, inc=1, device_id=((ctx + k) % ctx_count, head), device_id_type=MESH
        )
    pl.semaphore_wait(barrier, head_count + ctx_count - 2)

    def slot(back):
        return (BACK - back) * 2 + c

    x_peer = (ctx, (1 - x) * 2 + c)
    y_peer = (z * 2 + 1 - y, head)
    z_next = ((ctx + 2) % ctx_count, head)
    sibling = (ctx, x * 2 + 1 - c)
    x_step = 1 - 2 * x
    y_step = 2 - 4 * y

    def link(event, src, back, device):
        return pltpu.make_async_remote_copy(
            src_ref=src, dst_ref=win_ref.at[slot(back)], send_sem=send_sem.at[event],
            recv_sem=recv_sem.at[event], device_id=device, device_id_type=MESH,
        )

    def held(back):
        return win_ref.at[slot(back)]

    last_z = z >= ctx_count // 2 - 1
    sends = {
        Z1: (~last_z, lambda: link(Z1, kv_ref, 4, z_next)),
        X0: (x == 0, lambda: link(X0, kv_ref, 1, x_peer)),
        Y0: (y == 0, lambda: link(Y0, kv_ref, 2, y_peer)),
        Z2: ((z >= 1) & ~last_z, lambda: link(Z2, held(4), 8, z_next)),
        X1: (z >= 1, lambda: link(X1, held(4), 4 + x_step, x_peer)),
        Y1: (z >= 1, lambda: link(Y1, held(4), 4 + y_step, y_peer)),
        X2: ((z >= 2) & (x == 1), lambda: link(X2, held(8), 7, x_peer)),
        Y2: ((z >= 2) & (y == 1), lambda: link(Y2, held(8), 6, y_peer)),
        D0: (y == 1, lambda: link(D0, held(2), 2 + x_step, x_peer)),
        D1: (z >= 1, lambda: link(D1, held(4 - x_step), 4 - x_step + y_step, y_peer)),
        D2: ((z >= 2) & (y == 0), lambda: link(D2, held(6), 6 + x_step, x_peer)),
    }
    arrivals = {
        X0: (x == 1, 1),
        X1: (z >= 1, 4 - x_step),
        X2: ((z >= 2) & (x == 0), 7),
        Y0: (y == 1, 2),
        Y1: (z >= 1, 4 - y_step),
        Y2: ((z >= 2) & (y == 0), 6),
        Z1: (z >= 1, 4),
        Z2: (z >= 2, 8),
        D0: (y == 1, 2 - x_step),
        D1: (z >= 1, 4 - x_step - y_step),
        D2: ((z >= 2) & (y == 0), 6 - x_step),
    }

    def pair(event):
        back = 0 if event == OWN else arrivals[event][1]
        src = kv_ref if event == OWN else held(back)
        return pltpu.make_async_remote_copy(
            src_ref=src, dst_ref=held(back), send_sem=pair_send.at[event],
            recv_sem=pair_recv.at[event], device_id=sibling, device_id_type=MESH,
        )

    def start(event):
        condition, make = sends[event]

        @pl.when(condition)
        def _():
            make().start()

    def arrive(event, *then):
        condition, back = arrivals[event]

        @pl.when(condition)
        def _():
            link(event, kv_ref, back, sibling).wait_recv()
            for other in then:
                start(other)
            pair(event).start()

    def head_copy(k):
        peer = (head + k) % head_count
        return pltpu.make_async_remote_copy(
            src_ref=att_ref.at[:, pl.ds(pl.multiple_of(peer * cols, cols), cols)],
            dst_ref=gathered.at[head], send_sem=head_send.at[k], recv_sem=head_recv.at[k],
            device_id=(ctx, peer), device_id_type=MESH,
        )

    def ctx_copy(k):
        peer = (ctx + k) % ctx_count
        return pltpu.make_async_remote_copy(
            src_ref=outgoing.at[peer], dst_ref=short_ref.at[ctx], send_sem=ctx_send.at[k],
            recv_sem=ctx_recv.at[k], device_id=(peer, head), device_id_type=MESH,
        )

    for k in range(1, head_count):
        head_copy(k).start()
    own_att = pltpu.make_async_copy(
        att_ref.at[:, pl.ds(pl.multiple_of(head * cols, cols), cols)], gathered.at[head],
        local_sem.at[0],
    )
    own_att.start()
    for event in (Z1, X0, Y0):
        start(event)
    pair(OWN).start()
    own_kv = pltpu.make_async_copy(kv_ref, held(0), local_sem.at[1])
    own_kv.start()

    def fill(index):
        return pltpu.make_async_copy(kv_ref, win_ref.at[index], fill_sem.at[index])

    for index in range(2 * BACK):

        @pl.when(chip < BACK - index // 2)
        def _(index=index):
            fill(index).start()

    own_att.wait()
    for k in range(1, head_count):
        head_copy(k).wait_recv()
    for e in range(ctx_count):
        placed = jnp.zeros(gathered.shape[1:], gathered.dtype)
        for g in range(head_count):
            placed = jnp.where(dest_ref[0, g] == e, gathered[g], placed)
        outgoing[e] = placed
    for k in range(1, ctx_count):
        ctx_copy(k).start()
    own_short = pltpu.make_async_copy(outgoing.at[ctx], short_ref.at[ctx], local_sem.at[2])
    own_short.start()

    arrive(Y0, D0)
    arrive(X0)
    arrive(Z1, Z2, X1, Y1)
    arrive(Z2, X2, Y2)
    arrive(X1, D1)
    arrive(Y2, D2)
    for event in (Y1, X2, D0, D1, D2):
        arrive(event)

    pair(OWN).wait()
    for event in range(OWN):

        @pl.when(sends[event][0])
        def _(event=event):
            sends[event][1]().wait_send()

        @pl.when(arrivals[event][0])
        def _(event=event):
            pair(event).wait()

    own_kv.wait()
    own_short.wait()
    for index in range(2 * BACK):

        @pl.when(chip < BACK - index // 2)
        def _(index=index):
            fill(index).wait()

    for k in range(1, head_count):
        head_copy(k).wait_send()
    for k in range(1, ctx_count):
        ctx_copy(k).wait()


def exchange(kv, att, dest):
    ctx_count, head_count = lax.axis_size("ctx"), lax.axis_size("head")
    cols = att.shape[1] // head_count
    dma = pltpu.SemaphoreType.DMA
    return pl.pallas_call(
        exchange_kernel,
        out_shape=(
            jax.ShapeDtypeStruct((SLOTS, CHUNK, kv.shape[1]), jnp.bfloat16),
            jax.ShapeDtypeStruct((ctx_count, SCAP, cols), jnp.bfloat16),
        ),
        in_specs=[
            pl.BlockSpec(memory_space=pl.ANY),
            pl.BlockSpec(memory_space=pl.ANY),
            pl.BlockSpec(memory_space=pltpu.SMEM),
        ],
        out_specs=(pl.BlockSpec(memory_space=pl.ANY), pl.BlockSpec(memory_space=pl.ANY)),
        scratch_shapes=[
            pltpu.VMEM((head_count, SCAP, cols), jnp.bfloat16),
            pltpu.VMEM((ctx_count, SCAP, cols), jnp.bfloat16),
            dma((12,)), dma((12,)), dma((12,)), dma((12,)),
            dma((head_count,)), dma((head_count,)), dma((ctx_count,)), dma((ctx_count,)),
            dma((3,)), dma((2 * BACK,)),
        ],
        compiler_params=pltpu.CompilerParams(
            collective_id=0, has_side_effects=True, vmem_limit_bytes=16 * MIB
        ),
        cost_estimate=pl.CostEstimate(flops=0, bytes_accessed=40 * MIB, transcendentals=0),
    )(kv, att, dest)


def place_groups(dest, rows_array, groups, ctx_count):
    shaped = rows_array.reshape(groups, SCAP, rows_array.shape[1])
    hit = dest[None, :] == jnp.arange(ctx_count, dtype=jnp.int32)[:, None]
    which = jnp.argmax(hit, axis=1)
    return jnp.where(jnp.any(hit, axis=1)[:, None, None], shaped[which], 0)


def per_device(long_q, long_kv, long_lengths, short_q, short_kv, short_docs, short_dest):
    ctx_count, head_count = lax.axis_size("ctx"), lax.axis_size("head")
    rows = long_q.shape[0]

    def rank():
        return lax.axis_index("ctx") * head_count + lax.axis_index("head")

    def first_row_of():
        return rank() * rows

    short_att = short_attention(short_q, short_kv, short_docs)
    if ctx_count == 8 and head_count == 4 and rows == CHUNK and short_q.shape[0] == SCAP:

        def base_of():
            return (rank() // 2 - BACK) * 2 * CHUNK

        window, short_out = exchange(long_kv, short_att, short_dest)
        window = window.reshape(WINDOW, long_kv.shape[1])
        short_out = short_out.reshape(ctx_count * SCAP, -1)
    else:

        def base_of():
            return jnp.maximum(first_row_of() + rows - WINDOW, 0)

        everything = lax.all_gather(long_kv, ("ctx", "head"), axis=0, tiled=True)
        window = lax.dynamic_slice_in_dim(everything, base_of(), WINDOW, 0)
        gathered = lax.all_to_all(short_att, "head", split_axis=1, concat_axis=0, tiled=True)
        placed = place_groups(short_dest[0], gathered, short_dest.shape[1], ctx_count)
        arrived = lax.all_to_all(placed, "ctx", split_axis=0, concat_axis=0, tiled=True)
        short_out = arrived.reshape(ctx_count * SCAP, -1)
    long_out = long_attention(first_row_of, base_of, long_lengths, long_q, window)
    return (long_out, short_out)


def solution(mesh):
    in_specs = (
        P(("ctx", "head"), None),
        P(("ctx", "head"), None),
        P(),
        P(("ctx", "head"), None),
        P(("ctx", "head"), None),
        P("ctx", None),
        P("ctx", None),
    )
    out_specs = (P(("ctx", "head"), None), P("ctx", "head"))
    return jax.shard_map(
        per_device, mesh=mesh, in_specs=in_specs, out_specs=out_specs, check_vma=False
    )
```

```python
import functools

import jax
import jax.numpy as jnp
from jax import lax
from jax.experimental import pallas as pl
from jax.experimental.pallas import tpu as pltpu
from jax.sharding import PartitionSpec as P

H = 64
KV = 8
HD = 128
SCAP = 32
LMAX = 2048
GROUP = H // KV
CHUNK = 128
BACK = 8
PIECES = 4
PART = CHUNK // PIECES
HEADS = 2
SLOTS = 2 * (BACK + 1)
WINDOW = SLOTS * CHUNK
FAR = BACK
NEAR = SLOTS - FAR
LOG2E = 1.4426950408889634
EXP_SCALE = LOG2E * HD ** (-0.5)
masked_score = -1e30
MESH = pl.DeviceIdType.MESH
MIB = 1024 * 1024


def stacked_queries(q_ref, first_row, rows, first_head, heads):
    parts = [
        q_ref[first_row : first_row + rows, (first_head + g) * HD : (first_head + g + 1) * HD]
        for g in range(heads)
    ]
    return jnp.concatenate(parts, axis=0)


def attend(queries, keys, values, bias):
    scores = (
        lax.dot_general(
            queries, keys, (((1,), (1,)), ((), ())), preferred_element_type=jnp.float32
        )
        + bias
    )
    top = jnp.max(scores, axis=1, keepdims=True)
    weight = jnp.exp2((scores - top) * EXP_SCALE)
    total = jnp.sum(weight, axis=1, keepdims=True)
    out = jnp.dot(weight.astype(jnp.bfloat16), values, preferred_element_type=jnp.float32)
    return (out / total).astype(jnp.bfloat16)


def long_kernel(first_row_of, base_of, len_ref, q_ref, kv_ref, out_ref, bias_ref):
    rows = q_ref.shape[0]
    window = kv_ref.shape[0]

    @pl.when(pl.program_id(0) == 0)
    def _():
        query_pos = first_row_of() + lax.broadcasted_iota(jnp.int32, (rows, 1), 0)
        doc_start = jnp.zeros((rows, 1), jnp.int32)
        end = jnp.int32(0)
        for i in range(len_ref.shape[0]):
            end = end + len_ref[i]
            doc_start = jnp.where(query_pos >= end, end, doc_start)
        key_pos = base_of() + lax.broadcasted_iota(jnp.int32, (rows, window), 1)
        visible = (key_pos <= query_pos) & (key_pos >= doc_start)
        bias_ref[...] = jnp.where(visible, 0.0, masked_score)

    heads = 256 // rows
    keys = kv_ref[:, :HD]
    values = kv_ref[:, HD:]
    for block in range(GROUP // heads):
        first = block * heads
        queries = stacked_queries(q_ref, 0, rows, first, heads)
        bias = jnp.concatenate([bias_ref[...]] * heads, axis=0)
        out = attend(queries, keys, values, bias)
        for g in range(heads):
            out_ref[:, (first + g) * HD : (first + g + 1) * HD] = out[g * rows : (g + 1) * rows]


def long_attention(first_row_of, base_of, lengths, q, window):
    rows, keys = q.shape[0], window.shape[0]
    scores = H * rows * keys
    return pl.pallas_call(
        functools.partial(long_kernel, first_row_of, base_of),
        grid=(KV,),
        out_shape=jax.ShapeDtypeStruct(q.shape, jnp.bfloat16),
        in_specs=[
            pl.BlockSpec(memory_space=pltpu.SMEM),
            pl.BlockSpec((rows, GROUP * HD), lambda h: (0, h)),
            pl.BlockSpec((keys, 2 * HD), lambda h: (0, h)),
        ],
        out_specs=pl.BlockSpec((rows, GROUP * HD), lambda h: (0, h)),
        scratch_shapes=[pltpu.VMEM((rows, keys), jnp.float32)],
        compiler_params=pltpu.CompilerParams(vmem_limit_bytes=50 * MIB),
        cost_estimate=pl.CostEstimate(
            flops=4 * HD * scores, bytes_accessed=4 * q.size + 2 * window.size, transcendentals=scores
        ),
    )(lengths, q, window)


def short_kernel(q_ref, kv_ref, docs_ref, out_ref):
    groups = q_ref.shape[0] // SCAP
    first_group = lax.axis_index("head") * groups
    row = lax.broadcasted_iota(jnp.int32, (SCAP, SCAP), 0)
    col = lax.broadcasted_iota(jnp.int32, (SCAP, SCAP), 1)
    for j in range(groups):
        key_doc = jnp.broadcast_to(docs_ref[pl.ds(first_group + j, 1), :], (SCAP, SCAP))
        query_doc = jnp.sum(jnp.where(row == col, key_doc, 0), axis=1, keepdims=True)
        visible = (key_doc == query_doc) & (col <= row)
        bias = jnp.concatenate([jnp.where(visible, 0.0, masked_score)] * GROUP, axis=0)
        rows = slice(j * SCAP, (j + 1) * SCAP)
        for h in range(KV):
            out = attend(
                stacked_queries(q_ref, j * SCAP, SCAP, h * GROUP, GROUP),
                kv_ref[rows, 2 * h * HD : (2 * h + 1) * HD],
                kv_ref[rows, (2 * h + 1) * HD : (2 * h + 2) * HD],
                bias,
            )
            for g in range(GROUP):
                head = h * GROUP + g
                out_ref[rows, head * HD : (head + 1) * HD] = out[g * SCAP : (g + 1) * SCAP]


def short_attention(q, kv, docs):
    return pl.pallas_call(
        short_kernel,
        out_shape=jax.ShapeDtypeStruct(q.shape, jnp.bfloat16),
        in_specs=[pl.BlockSpec(memory_space=pltpu.VMEM)] * 3,
        out_specs=pl.BlockSpec(memory_space=pltpu.VMEM),
        compiler_params=pltpu.CompilerParams(vmem_limit_bytes=32 * MIB),
    )(q, kv, docs)


X0, X1, X2, Y0, Y1, Y2, Z1, Z2, D0, D1, D2, OWN = range(12)


def exchange_kernel(
    len_ref, dest_ref, q_ref, kv_ref, att_ref, long_ref, short_ref,
    win_ref, acc_ref, top_ref, total_ref, start_ref, bias_ref, gathered, outgoing,
    send_sem, recv_sem, pair_send, pair_recv, head_send, head_recv, ctx_send, ctx_recv,
    local_sem, fill_sem,
):
    ctx, head = lax.axis_index("ctx"), lax.axis_index("head")
    ctx_count, head_count = lax.axis_size("ctx"), lax.axis_size("head")
    z, y, x, c = ctx // 2, ctx % 2, head // 2, head % 2
    chip = ctx * 2 + x
    cols = gathered.shape[2]

    barrier = pltpu.get_barrier_semaphore()
    for k in range(1, head_count):
        pl.semaphore_signal(
            barrier, inc=1, device_id=(ctx, (head + k) % head_count), device_id_type=MESH
        )
    for k in range(1, ctx_count):
        pl.semaphore_signal(
            barrier, inc=1, device_id=((ctx + k) % ctx_count, head), device_id_type=MESH
        )
    pl.semaphore_wait(barrier, head_count + ctx_count - 2)

    def slot(back):
        return (BACK - back) * 2 + c

    x_peer = (ctx, (1 - x) * 2 + c)
    y_peer = (z * 2 + 1 - y, head)
    z_next = ((ctx + 2) % ctx_count, head)
    sibling = (ctx, x * 2 + 1 - c)
    x_step = 1 - 2 * x
    y_step = 2 - 4 * y

    def part(ref, p):
        return ref.at[pl.ds(p * PART, PART)]

    def link(event, p, src, back, device):
        return pltpu.make_async_remote_copy(
            src_ref=part(src, p), dst_ref=part(win_ref.at[slot(back)], p),
            send_sem=send_sem.at[event, p], recv_sem=recv_sem.at[event, p],
            device_id=device, device_id_type=MESH,
        )

    def held(back):
        return win_ref.at[slot(back)]

    last_z = z >= ctx_count // 2 - 1
    sends = {
        Z1: (~last_z, lambda p: link(Z1, p, kv_ref, 4, z_next)),
        X0: (x == 0, lambda p: link(X0, p, kv_ref, 1, x_peer)),
        Y0: (y == 0, lambda p: link(Y0, p, kv_ref, 2, y_peer)),
        Z2: ((z >= 1) & ~last_z, lambda p: link(Z2, p, held(4), 8, z_next)),
        X1: (z >= 1, lambda p: link(X1, p, held(4), 4 + x_step, x_peer)),
        Y1: (z >= 1, lambda p: link(Y1, p, held(4), 4 + y_step, y_peer)),
        X2: ((z >= 2) & (x == 1), lambda p: link(X2, p, held(8), 7, x_peer)),
        Y2: ((z >= 2) & (y == 1), lambda p: link(Y2, p, held(8), 6, y_peer)),
        D0: (y == 1, lambda p: link(D0, p, held(2), 2 + x_step, x_peer)),
        D1: (z >= 1, lambda p: link(D1, p, held(4 - x_step), 4 - x_step + y_step, y_peer)),
        D2: ((z >= 2) & (y == 0), lambda p: link(D2, p, held(6), 6 + x_step, x_peer)),
    }
    arrivals = {
        X0: (x == 1, 1),
        X1: (z >= 1, 4 - x_step),
        X2: ((z >= 2) & (x == 0), 7),
        Y0: (y == 1, 2),
        Y1: (z >= 1, 4 - y_step),
        Y2: ((z >= 2) & (y == 0), 6),
        Z1: (z >= 1, 4),
        Z2: (z >= 2, 8),
        D0: (y == 1, 2 - x_step),
        D1: (z >= 1, 4 - x_step - y_step),
        D2: ((z >= 2) & (y == 0), 6 - x_step),
    }

    def pair(event, p):
        back = 0 if event == OWN else arrivals[event][1]
        src = kv_ref if event == OWN else held(back)
        return pltpu.make_async_remote_copy(
            src_ref=part(src, p), dst_ref=part(held(back), p), send_sem=pair_send.at[event, p],
            recv_sem=pair_recv.at[event, p], device_id=sibling, device_id_type=MESH,
        )

    def start(event, p):
        condition, make = sends[event]

        @pl.when(condition)
        def _():
            make(p).start()

    def arrive(p, event, *then):
        condition, back = arrivals[event]

        @pl.when(condition)
        def _():
            link(event, p, kv_ref, back, sibling).wait_recv()
            for other in then:
                start(other, p)
            pair(event, p).start()

    first_row = (ctx * head_count + head) * CHUNK

    def find_starts():
        query_pos = first_row + lax.broadcasted_iota(jnp.int32, (CHUNK, HD), 0)
        doc_start = jnp.zeros((CHUNK, HD), jnp.int32)
        end = jnp.int32(0)
        for i in range(len_ref.shape[0]):
            end = end + len_ref[i]
            doc_start = jnp.where(query_pos >= end, end, doc_start)
        start_ref[...] = doc_start

    def set_bias(first_slot, slots):
        query_pos = first_row + lax.broadcasted_iota(jnp.int32, (CHUNK, HD), 0)
        for index in range(slots):
            key_pos = (
                (chip - BACK) * 2 * CHUNK
                + (first_slot + index) * CHUNK
                + lax.broadcasted_iota(jnp.int32, (CHUNK, HD), 1)
            )
            visible = (key_pos <= query_pos) & (key_pos >= start_ref[...])
            bias_ref[:, index * CHUNK : (index + 1) * CHUNK] = jnp.where(
                visible, 0.0, masked_score
            )

    def attend_slots(first_slot, slots, merge, from_head, to_head):
        def one(h, carry):
            key_cols = pl.ds(pl.multiple_of(h * 2 * HD, HD), HD)
            value_cols = pl.ds(pl.multiple_of((h * 2 + 1) * HD, HD), HD)
            which = pl.ds(first_slot, slots)
            keys = win_ref[which, :, key_cols].reshape(slots * CHUNK, HD)
            values = win_ref[which, :, value_cols].reshape(slots * CHUNK, HD)
            for block in range(GROUP // HEADS):
                first_head = h * GROUP + block * HEADS
                queries = jnp.concatenate(
                    [
                        q_ref[:, pl.ds(pl.multiple_of((first_head + g) * HD, HD), HD)]
                        for g in range(HEADS)
                    ],
                    axis=0,
                )
                bias = jnp.concatenate([bias_ref[:, : slots * CHUNK]] * HEADS, axis=0)
                scores = (
                    lax.dot_general(
                        queries, keys, (((1,), (1,)), ((), ())), preferred_element_type=jnp.float32
                    )
                    + bias
                )
                rows = pl.ds(block * HEADS * CHUNK, HEADS * CHUNK)
                shape = (HEADS * CHUNK, HD)
                top = jnp.max(scores, axis=1, keepdims=True)
                weight = jnp.exp2((scores - top) * EXP_SCALE)
                total = jnp.sum(weight, axis=1, keepdims=True)
                numerator = jnp.dot(
                    weight.astype(jnp.bfloat16), values, preferred_element_type=jnp.float32
                )
                top = jnp.broadcast_to(top, shape)
                total = jnp.broadcast_to(total, shape)
                if not merge:
                    top_ref[h, rows, :] = top
                    total_ref[h, rows, :] = total
                    acc_ref[h, rows, :] = numerator
                else:
                    before = top_ref[h, rows, :]
                    both = jnp.maximum(before, top)
                    factor = jnp.exp2((before - both) * EXP_SCALE)
                    scale = jnp.exp2((top - both) * EXP_SCALE)
                    total = total_ref[h, rows, :] * factor + total * scale
                    numerator = acc_ref[h, rows, :] * factor + numerator * scale
                    out = (numerator / total).astype(jnp.bfloat16)
                    for g in range(HEADS):
                        cols_of = pl.ds(pl.multiple_of((first_head + g) * HD, HD), HD)
                        long_ref[:, cols_of] = out[g * CHUNK : (g + 1) * CHUNK]
            return carry

        lax.fori_loop(from_head, to_head, one, 0)

    def ready(event):
        @pl.when(arrivals[event][0])
        def _():
            for p in range(PIECES):
                pair(event, p).wait_recv()

    def finish():
        def one(h, carry):
            for g in range(GROUP):
                rows = pl.ds(g * CHUNK, CHUNK)
                cols_of = pl.ds(pl.multiple_of((h * GROUP + g) * HD, HD), HD)
                long_ref[:, cols_of] = (acc_ref[h, rows, :] / total_ref[h, rows, :]).astype(
                    jnp.bfloat16
                )
            return carry

        lax.fori_loop(0, KV, one, 0)

    def head_copy(k):
        peer = (head + k) % head_count
        return pltpu.make_async_remote_copy(
            src_ref=att_ref.at[:, pl.ds(pl.multiple_of(peer * cols, cols), cols)],
            dst_ref=gathered.at[head], send_sem=head_send.at[k], recv_sem=head_recv.at[k],
            device_id=(ctx, peer), device_id_type=MESH,
        )

    def ctx_copy(k):
        peer = (ctx + k) % ctx_count
        return pltpu.make_async_remote_copy(
            src_ref=outgoing.at[peer], dst_ref=short_ref.at[ctx], send_sem=ctx_send.at[k],
            recv_sem=ctx_recv.at[k], device_id=(peer, head), device_id_type=MESH,
        )

    for k in range(1, head_count):
        head_copy(k).start()
    own_att = pltpu.make_async_copy(
        att_ref.at[:, pl.ds(pl.multiple_of(head * cols, cols), cols)], gathered.at[head],
        local_sem.at[0],
    )
    own_att.start()
    for p in range(PIECES):
        for event in (Z1, X0, Y0):
            start(event, p)
    for p in range(PIECES):
        pair(OWN, p).start()
    own_kv = pltpu.make_async_copy(kv_ref, held(0), local_sem.at[1])
    own_kv.start()

    def fill(index):
        return pltpu.make_async_copy(kv_ref, win_ref.at[index], fill_sem.at[index])

    for index in range(2 * BACK):

        @pl.when(chip < BACK - index // 2)
        def _(index=index):
            fill(index).start()

    find_starts()
    set_bias(FAR, NEAR)
    for p in range(PIECES):
        arrive(p, Z1, Z2, X1, Y1)
        arrive(p, Y0, D0)
        arrive(p, X0)
    for p in range(PIECES):
        arrive(p, Z2, X2, Y2)
        arrive(p, X1, D1)

    own_att.wait()
    for k in range(1, head_count):
        head_copy(k).wait_recv()
    for e in range(ctx_count):
        placed = jnp.zeros(gathered.shape[1:], gathered.dtype)
        for g in range(head_count):
            placed = jnp.where(dest_ref[0, g] == e, gathered[g], placed)
        outgoing[e] = placed
    own_short = pltpu.make_async_copy(outgoing.at[ctx], short_ref.at[ctx], local_sem.at[2])
    own_short.start()

    for event in (Y1, D0, D1):
        for p in range(PIECES):
            arrive(p, event)
    for index in range(2 * BACK):

        @pl.when(chip < BACK - index // 2)
        def _(index=index):
            fill(index).wait()

    own_kv.wait()
    for p in range(PIECES):
        pair(OWN, p).wait_recv()
    for event in (X0, Y0, Z1, X1, Y1, D0, D1):
        ready(event)
    for k in range(1, ctx_count):
        ctx_copy(k).start()
    for p in range(PIECES):
        attend_slots(FAR, NEAR, False, p, p + 1)
        arrive(p, Y2, D2)
    for p in range(PIECES):
        arrive(p, X2)
    attend_slots(FAR, NEAR, False, KV // 2, KV)
    for p in range(PIECES):
        arrive(p, D2)
    for event in (Z2, X2, Y2, D2):
        ready(event)

    @pl.when(chip > BACK // 2)
    def _():
        set_bias(0, FAR)
        attend_slots(0, FAR, True, 0, KV)

    @pl.when(chip <= BACK // 2)
    def _():
        finish()

    for p in range(PIECES):
        pair(OWN, p).wait_send()
        for event in range(OWN):

            @pl.when(sends[event][0])
            def _(event=event, p=p):
                sends[event][1](p).wait_send()

            @pl.when(arrivals[event][0])
            def _(event=event, p=p):
                pair(event, p).wait_send()

    own_short.wait()
    for k in range(1, head_count):
        head_copy(k).wait_send()
    for k in range(1, ctx_count):
        ctx_copy(k).wait()


def exchange(lengths, dest, q, kv, att):
    ctx_count, head_count = lax.axis_size("ctx"), lax.axis_size("head")
    cols = att.shape[1] // head_count
    dma = pltpu.SemaphoreType.DMA
    scores = H * CHUNK * WINDOW
    state = pltpu.VMEM((KV, GROUP * CHUNK, HD), jnp.float32)
    return pl.pallas_call(
        exchange_kernel,
        out_shape=(
            jax.ShapeDtypeStruct(q.shape, jnp.bfloat16),
            jax.ShapeDtypeStruct((ctx_count, SCAP, cols), jnp.bfloat16),
        ),
        in_specs=[
            pl.BlockSpec(memory_space=pltpu.SMEM),
            pl.BlockSpec(memory_space=pltpu.SMEM),
            pl.BlockSpec(memory_space=pltpu.VMEM),
            pl.BlockSpec(memory_space=pl.ANY),
            pl.BlockSpec(memory_space=pl.ANY),
        ],
        out_specs=(pl.BlockSpec(memory_space=pltpu.VMEM), pl.BlockSpec(memory_space=pl.ANY)),
        scratch_shapes=[
            pltpu.VMEM((SLOTS, CHUNK, kv.shape[1]), jnp.bfloat16),
            state, state, state,
            pltpu.VMEM((CHUNK, HD), jnp.int32),
            pltpu.VMEM((CHUNK, NEAR * CHUNK), jnp.float32),
            pltpu.VMEM((head_count, SCAP, cols), jnp.bfloat16),
            pltpu.VMEM((ctx_count, SCAP, cols), jnp.bfloat16),
            dma((12, PIECES)), dma((12, PIECES)), dma((12, PIECES)), dma((12, PIECES)),
            dma((head_count,)), dma((head_count,)), dma((ctx_count,)), dma((ctx_count,)),
            dma((3,)), dma((2 * BACK,)),
        ],
        compiler_params=pltpu.CompilerParams(
            collective_id=0, has_side_effects=True, vmem_limit_bytes=50 * MIB
        ),
        cost_estimate=pl.CostEstimate(
            flops=4 * HD * scores, bytes_accessed=16 * MIB, transcendentals=scores
        ),
    )(lengths, dest, q, kv, att)


def place_groups(dest, rows_array, groups, ctx_count):
    shaped = rows_array.reshape(groups, SCAP, rows_array.shape[1])
    hit = dest[None, :] == jnp.arange(ctx_count, dtype=jnp.int32)[:, None]
    which = jnp.argmax(hit, axis=1)
    return jnp.where(jnp.any(hit, axis=1)[:, None, None], shaped[which], 0)


def per_device(long_q, long_kv, long_lengths, short_q, short_kv, short_docs, short_dest):
    ctx_count, head_count = lax.axis_size("ctx"), lax.axis_size("head")
    rows = long_q.shape[0]

    def rank():
        return lax.axis_index("ctx") * head_count + lax.axis_index("head")

    def first_row_of():
        return rank() * rows

    short_att = short_attention(short_q, short_kv, short_docs)
    if ctx_count == 8 and head_count == 4 and rows == CHUNK and short_q.shape[0] == SCAP:
        long_out, short_out = exchange(long_lengths, short_dest, long_q, long_kv, short_att)
        return (long_out, short_out.reshape(ctx_count * SCAP, -1))

    def base_of():
        return jnp.maximum(first_row_of() + rows - WINDOW, 0)

    everything = lax.all_gather(long_kv, ("ctx", "head"), axis=0, tiled=True)
    window = lax.dynamic_slice_in_dim(everything, base_of(), WINDOW, 0)
    gathered = lax.all_to_all(short_att, "head", split_axis=1, concat_axis=0, tiled=True)
    placed = place_groups(short_dest[0], gathered, short_dest.shape[1], ctx_count)
    arrived = lax.all_to_all(placed, "ctx", split_axis=0, concat_axis=0, tiled=True)
    short_out = arrived.reshape(ctx_count * SCAP, -1)
    long_out = long_attention(first_row_of, base_of, long_lengths, long_q, window)
    return (long_out, short_out)


def solution(mesh):
    in_specs = (
        P(("ctx", "head"), None),
        P(("ctx", "head"), None),
        P(),
        P(("ctx", "head"), None),
        P(("ctx", "head"), None),
        P("ctx", None),
        P("ctx", None),
    )
    out_specs = (P(("ctx", "head"), None), P("ctx", "head"))
    return jax.shard_map(
        per_device, mesh=mesh, in_specs=in_specs, out_specs=out_specs, check_vma=False
    )
```
